32 devices in a mesh: groups: 2 (over y), row: 8 (over z, x), col: 2 (over core).
Axes of the slice: x: 2, y: 2, z: 4, core: 2. Of those that a mesh axis runs over, the one named last changes fastest.
Arguments:
- concentration: float32 [512, 256, 256], P('groups', 'row', 'col'), parts along dimension 0, may hold values from -6 to 6
- species: int32 [2], P('groups'), parts along dimension 0, may hold values from 0 to 63
- reaction_rates: float32 [64], replicated, may hold values from 0.2 to 0.8
- levels: float32 [64], replicated, may hold values from -1 to 1
- sweep_flags: int32 [2, 3], replicated, may hold values from 0 to 1
- explicit_line: float32 [256, 256], replicated, may hold values from -0.5 to 1.2
- inverse_line: float32 [256, 256], replicated, may hold values from -0.5 to 1.2
- explicit_depth: float32 [256, 256], replicated, may hold values from -0.5 to 1.2
- inverse_depth: float32 [256, 256], replicated, may hold values from -0.5 to 1.2
Outputs:
- advanced: float32 [512, 256, 256], P('groups', 'row', 'col'), parts along dimension 0
The draws below stay inside these ranges and needn't reach their ends.
There are 2 independent parts, one for each index of `groups`. The reference program is written for one: setup_inputs(seed, part) draws one part's arguments, and reference() takes and returns one part's arrays. A program takes and returns all parts, laid end to end along the dimension named above; an argument that names none is the same for every part. Nothing has to cross between parts.
All inputs are finite; a program needn't handle non-finite values.
Results may differ from the reference program's by a relative error of at most 0.00011.
Values sent between devices are 32-bit elements; how exact they have to be, the bound alone decides.
No kernel may reach another device: no remote copies, remote signals or barrier semaphores. Data moves between devices by JAX's collectives and lax.ppermute only.
A program may use at most 64 MiB of HBM per device.

```python
import math
import jax
import jax.numpy as jnp
from jax import lax

NL = 256
NZ = 256
STEPS = 2
SPECIES = 64


def build_operator(key, order_size, lowest, highest):
    key_diagonal, key_spread = jax.random.split(key)
    diagonal_part = jax.random.uniform(key_diagonal, (order_size,), jnp.float32, lowest, highest)
    spread_part = jnp.clip(jax.random.normal(key_spread, (order_size, order_size), jnp.float32), -3.0, 3.0)
    spread_part = spread_part * (0.3 / math.sqrt(order_size))
    return spread_part + jnp.diag(diagonal_part)


def draw_explicit_line(key, part):
    return build_operator(jax.random.fold_in(key, 11), NL, 0.9, 1.1)


def draw_inverse_line(key, part):
    return build_operator(jax.random.fold_in(key, 23), NL, 0.8, 1.0)


def draw_explicit_depth(key, part):
    return build_operator(jax.random.fold_in(key, 37), NZ, 0.9, 1.1)


def draw_inverse_depth(key, part):
    return build_operator(jax.random.fold_in(key, 41), NZ, 0.8, 1.0)


def touch_ends(result, stream_key, low, high):
    longest = result.shape.index(max(result.shape))
    spots = []
    for shift in (0, 1):
        where = [jax.random.randint(jax.random.fold_in(stream_key, axis), (), 0, length) for axis, length in enumerate(result.shape)]
        where[longest] = (where[longest] + shift) % result.shape[longest]
        spots.append(tuple(where))
    return result.at[spots[0]].set(low).at[spots[1]].set(high)


def block_scale(rng, dims, shards, least, high):
    def one(dim, parts):
        heights = jax.random.uniform(jax.random.fold_in(jax.random.fold_in(rng, 6), dim), (parts,), jnp.float32, least / len(shards), high / len(shards))
        return jnp.repeat(jnp.exp(heights), dims[dim] // parts).reshape((-1,) + (1,) * (len(dims) - dim - 1))

    factor_of = one(*shards[0])
    for cut in shards[1:]:
        factor_of = factor_of * one(*cut)
    return factor_of


def noise(key, dims, width, bound, shards=(), held_as=jnp.bfloat16):
    values = jax.random.normal(key, dims, jnp.float32) * width
    if len(shards) > 0:
        values = block_scale(key, dims, shards, -0.22, 0.18) * values
    return jnp.clip(values, min=-bound, max=bound).astype(held_as)


def setup_inputs(seed: int = 0, part: int = 0) -> dict:
    key_list = jax.random.split(jax.random.key(seed), 10)
    own_keys = jax.random.split(jax.random.fold_in(key_list[9], part), 10)
    return {
        "concentration": noise(own_keys[0], (NL, NL, NZ), 1.0, 6.0, ((1, 8), (2, 2)), jnp.float32),
        "species": jax.random.randint(own_keys[1], (1,), 0, SPECIES).astype(jnp.int32),
        "reaction_rates": jnp.clip(jnp.exp(jax.random.uniform(key_list[2], (SPECIES,), jnp.float32, math.log(0.2), math.log(0.8))), 0.2, 0.8),
        "levels": jnp.clip(jax.random.uniform(key_list[3], (SPECIES,), jnp.float32, -1.0, 1.0), -1.0, 1.0),
        "sweep_flags": touch_ends(jax.random.randint(key_list[4], (STEPS, 3), 0, 2), jax.random.fold_in(key_list[4], 1), 0, 1).astype(jnp.int32),
        "explicit_line": draw_explicit_line(jax.random.fold_in(key_list[9], 71), part),
        "inverse_line": draw_inverse_line(jax.random.fold_in(key_list[9], 71), part),
        "explicit_depth": draw_explicit_depth(jax.random.fold_in(key_list[9], 71), part),
        "inverse_depth": draw_inverse_depth(jax.random.fold_in(key_list[9], 71), part),
    }


def apply_line(matrix, field_now, axis_dim):
    if axis_dim == 0:
        return jnp.einsum("ij,jbc->ibc", matrix, field_now, precision=lax.Precision.HIGHEST)
    if axis_dim == 1:
        return jnp.einsum("ij,ajc->aic", matrix, field_now, precision=lax.Precision.HIGHEST)
    return jnp.einsum("ij,abj->abi", matrix, field_now, precision=lax.Precision.HIGHEST)


def oriented(matrix, reflect):
    return jnp.where(reflect == 1, matrix[::-1, ::-1], matrix)


def reference(concentration, species, reaction_rates, levels, sweep_flags, explicit_line, inverse_line, explicit_depth, inverse_depth):
    picker = (jnp.arange(reaction_rates.shape[0], dtype=jnp.int32) == species[0]).astype(jnp.float32)
    kinetic_rate = jnp.sum(reaction_rates * picker)
    equilibrium = jnp.sum(levels * picker)
    field_now = concentration
    for step_index in range(STEPS):
        order = [0, 1, 2] if step_index % 2 == 0 else [2, 1, 0]
        for axis_dim in order:
            if axis_dim < 2:
                explicit_now, inverse_now = explicit_line, inverse_line
            else:
                explicit_now, inverse_now = explicit_depth, inverse_depth
            reflect = sweep_flags[step_index, axis_dim]
            field_now = field_now - kinetic_rate * jnp.tanh(field_now - equilibrium)
            field_now = apply_line(oriented(explicit_now, reflect), field_now, axis_dim)
            field_now = apply_line(oriented(inverse_now, reflect), field_now, axis_dim)
    return field_now
```

```python
import functools
import jax
import jax.numpy as jnp
from jax import lax
from jax.experimental import pallas as pl
from jax.experimental.pallas import tpu as pltpu
from jax.sharding import PartitionSpec as P

F32 = jnp.float32
BF16 = jnp.bfloat16
CHUNKS = 2
VMEM_LIMIT = 48 * 1024 * 1024


def split(value):
    high = value.astype(BF16)
    return high, (value - high.astype(F32)).astype(BF16)


def product(left, right):
    dot = functools.partial(jnp.dot, preferred_element_type=F32)
    return dot(left[0], right[0]) + (dot(left[0], right[1]) + dot(left[1], right[0]))


def react(value, kinetics):
    rate, level = kinetics
    return value - rate * jnp.tanh(value - level)


def read_kinetics(species_ref, rates_ref, levels_ref):
    index = species_ref[0]
    return rates_ref[index], levels_ref[index]


def reversal(flag, size):
    rows = lax.broadcasted_iota(jnp.int32, (size, size), 0)
    columns = lax.broadcasted_iota(jnp.int32, (size, size), 1)
    target = jnp.where(flag == 1, size - 1 - rows, rows)
    return jnp.where(columns == target, 1.0, 0.0).astype(BF16)


def combined(inverse, explicit):
    return jnp.dot(inverse, explicit, precision=lax.Precision.HIGHEST, preferred_element_type=F32)


def orient(pieces, flag):
    turn = reversal(flag, pieces[0].shape[0])
    dot = functools.partial(jnp.dot, preferred_element_type=F32)
    return tuple(dot(dot(turn, piece).astype(BF16), turn).astype(BF16) for piece in pieces)


def first_sweep(chunk, species, rates, levels, flags, explicit, inverse, field, out, high, low):
    rows = high.shape[0]

    @pl.when(pl.program_id(0) == 0)
    def _():
        pieces = orient(split(combined(inverse[...], explicit[...])), flags[0, 0])
        high[...] = pieces[0][chunk * rows : (chunk + 1) * rows]
        low[...] = pieces[1][chunk * rows : (chunk + 1) * rows]

    kinetics = read_kinetics(species, rates, levels)
    matrix = (high[...], low[...])
    ranks, each, depth, width = out.shape
    for cell in range(0, depth, 2):
        value = jnp.concatenate([field[:, cell, :], field[:, cell + 1, :]], axis=1)
        result = product(matrix, split(react(value, kinetics)))
        for half in range(2):
            out[:, :, cell + half, :] = result[:, half * width : (half + 1) * width].reshape(
                ranks, each, width
            )


def last_sweep(chunk, species, rates, levels, flags, explicit, inverse, *refs):
    if chunk == 0:
        field, out, high, low = refs
    else:
        field, total, out, high, low = refs
    columns = high.shape[1]

    @pl.when(pl.program_id(0) == 0)
    def _():
        last = flags.shape[0] - 1
        pieces = orient(split(combined(inverse[...], explicit[...])), flags[last, 0])
        high[...] = pieces[0][:, chunk * columns : (chunk + 1) * columns]
        low[...] = pieces[1][:, chunk * columns : (chunk + 1) * columns]

    kinetics = read_kinetics(species, rates, levels)
    matrix = (high[...], low[...])
    ranks, each, depth, width = field.shape
    for cell in range(0, depth, 2):
        value = jnp.concatenate(
            [field[:, :, cell + half, :].reshape(ranks * each, width) for half in range(2)], axis=1
        )
        result = product(matrix, split(react(value, kinetics)))
        for half in range(2):
            part = result[:, half * width : (half + 1) * width]
            if chunk > 0:
                part = part + total[:, cell + half, :]
            out[:, cell + half, :] = part


def prepare(flags, explicit_line, inverse_line, explicit_depth, inverse_depth, high, low):
    line = split(combined(inverse_line[...], explicit_line[...]))
    depth = split(combined(inverse_depth[...], explicit_depth[...]).T)
    for place, (pieces, step, axis_dim) in enumerate(
        [(line, 0, 1), (depth, 0, 2), (depth, 1, 2), (line, 1, 1)]
    ):
        high[place], low[place] = orient(pieces, flags[step, axis_dim])


def plane_sweeps(rows, columns, species, rates, levels, high, low, field, out):
    kinetics = read_kinetics(species, rates, levels)
    each, depth, width = field.shape[1:]
    for cell in range(each):
        value = jnp.concatenate(
            [
                jnp.concatenate([field[r * columns + c, cell] for c in range(columns)], axis=1)
                for r in range(rows)
            ],
            axis=0,
        )
        for place in range(4):
            pieces = split(react(value, kinetics))
            matrix = (high[place], low[place])
            value = product(matrix, pieces) if place in (0, 3) else product(pieces, matrix)
        for r in range(rows):
            for c in range(columns):
                out[r * columns + c, cell] = value[
                    r * depth : (r + 1) * depth, c * width : (c + 1) * width
                ]


SMEM = pl.BlockSpec(memory_space=pltpu.SMEM)
WHOLE = pl.BlockSpec(memory_space=pltpu.VMEM)
PARAMS = pltpu.CompilerParams(vmem_limit_bytes=VMEM_LIMIT)


def cost(cells, length, sweeps, bytes_accessed):
    return pl.CostEstimate(
        flops=6 * cells * length * sweeps, bytes_accessed=bytes_accessed, transcendentals=cells * sweeps
    )


def fast(rows, columns, concentration, species, reaction_rates, levels, sweep_flags,
         explicit_line, inverse_line, explicit_depth, inverse_depth):
    lines, depth, width = concentration.shape
    ranks = rows * columns
    each = lines // ranks // CHUNKS
    block = 8
    kinetic = (species, reaction_rates, levels)
    size = lines * depth * width
    chunk_shape = jax.ShapeDtypeStruct((ranks, each, depth, width), F32)
    share = lines // CHUNKS

    def exchange(value):
        return lax.all_to_all(value, ("row", "col"), split_axis=0, concat_axis=0, tiled=True)

    chunk_spec = pl.BlockSpec((ranks, each, block, width), lambda i: (0, 0, i, 0))
    home_spec = pl.BlockSpec((lines, block, width), lambda i: (0, i, 0))

    def first(chunk):
        return pl.pallas_call(
            functools.partial(first_sweep, chunk),
            grid=(depth // block,),
            in_specs=[SMEM] * 4 + [WHOLE] * 2 + [home_spec],
            out_specs=chunk_spec,
            out_shape=chunk_shape,
            scratch_shapes=[pltpu.VMEM((share, lines), BF16)] * 2,
            compiler_params=PARAMS,
            cost_estimate=cost(size // CHUNKS, lines, 1, 4 * (size + size // CHUNKS)),
            name=f"first_sweep_{chunk}",
        )(*kinetic, sweep_flags, explicit_line, inverse_line, concentration)

    def planes(value, chunk):
        spec = pl.BlockSpec((ranks, 2, depth, width), lambda i: (0, i, 0, 0))
        return pl.pallas_call(
            functools.partial(plane_sweeps, rows, columns),
            grid=(each // 2,),
            in_specs=[SMEM] * 3 + [WHOLE] * 2 + [spec],
            out_specs=spec,
            out_shape=chunk_shape,
            compiler_params=PARAMS,
            cost_estimate=cost(size // CHUNKS, lines, 4, 8 * size // CHUNKS),
            name=f"plane_sweeps_{chunk}",
        )(*kinetic, high, low, value)

    def last(value, total, chunk):
        more = [] if chunk == 0 else [total]
        return pl.pallas_call(
            functools.partial(last_sweep, chunk),
            grid=(depth // block,),
            in_specs=[SMEM] * 4 + [WHOLE] * 2 + [chunk_spec] + [home_spec] * len(more),
            out_specs=home_spec,
            out_shape=jax.ShapeDtypeStruct((lines, depth, width), F32),
            scratch_shapes=[pltpu.VMEM((lines, share), BF16)] * 2,
            compiler_params=PARAMS,
            cost_estimate=cost(size // CHUNKS, lines, 1, 4 * (size + size // CHUNKS)),
            name=f"last_sweep_{chunk}",
        )(*kinetic, sweep_flags, explicit_line, inverse_line, value, *more)

    pieces_shape = jax.ShapeDtypeStruct((4, lines, lines), BF16)
    high, low = pl.pallas_call(
        prepare,
        in_specs=[SMEM] + [WHOLE] * 4,
        out_specs=[WHOLE] * 2,
        out_shape=[pieces_shape] * 2,
        compiler_params=PARAMS,
        cost_estimate=cost(lines * lines, lines, 8, 8 * 4 * lines * lines),
        name="prepare",
    )(sweep_flags, explicit_line, inverse_line, explicit_depth, inverse_depth)

    there = [exchange(first(chunk)) for chunk in range(CHUNKS)]
    back = [exchange(planes(there[chunk], chunk)) for chunk in range(CHUNKS)]
    total = None
    for chunk in range(CHUNKS):
        total = last(back[chunk], total, chunk)
    return total


def oriented(matrix, reflect):
    return jnp.where(reflect == 1, matrix[::-1, ::-1], matrix)


def plain(concentration, species, reaction_rates, levels, sweep_flags,
          explicit_line, inverse_line, explicit_depth, inverse_depth):
    kinetics = (reaction_rates[species[0]], levels[species[0]])
    matmul = functools.partial(jnp.einsum, precision=lax.Precision.HIGHEST)
    line = matmul("ij,jk->ik", inverse_line, explicit_line)
    deep = matmul("ij,jk->ik", inverse_depth, explicit_depth)
    letters = ["ij,jbc->ibc", "ij,ajc->aic", "ij,abj->abi"]

    def sweep(value, step, axis_dim):
        matrix = oriented(deep if axis_dim == 2 else line, sweep_flags[step, axis_dim])
        return matmul(letters[axis_dim], matrix, react(value, kinetics))

    def regroup(value):
        value = lax.all_to_all(value, "row", split_axis=0, concat_axis=1, tiled=True)
        return lax.all_to_all(value, "col", split_axis=0, concat_axis=2, tiled=True)

    def restore(value):
        value = lax.all_to_all(value, "col", split_axis=2, concat_axis=0, tiled=True)
        return lax.all_to_all(value, "row", split_axis=1, concat_axis=0, tiled=True)

    value, home = concentration, True
    for step in range(sweep_flags.shape[0]):
        for axis_dim in [0, 1, 2] if step % 2 == 0 else [2, 1, 0]:
            if home != (axis_dim == 0):
                value = restore(value) if axis_dim == 0 else regroup(value)
                home = axis_dim == 0
            value = sweep(value, step, axis_dim)
    return value if home else restore(value)


def solution(mesh):
    rows, columns = mesh.shape["row"], mesh.shape["col"]

    def on_device(*args):
        lines, depth, width = args[0].shape
        fits = (
            args[4].shape[0] == 2
            and lines % (rows * columns * CHUNKS * 8) == 0
            and depth % 8 == 0
            and width % 128 == 0
            and depth * rows == lines
            and width * columns == args[7].shape[0] == lines
        )
        if fits:
            return fast(rows, columns, *args)
        return plain(*args)

    in_specs = (P("groups", "row", "col"), P("groups"), P(), P(), P(), P(), P(), P(), P())
    return jax.shard_map(
        on_device, mesh=mesh, in_specs=in_specs, out_specs=P("groups", "row", "col"), check_vma=False
    )
```

```python
import functools
import jax
import jax.numpy as jnp
from jax import lax
from jax.experimental import pallas as pl
from jax.experimental.pallas import tpu as pltpu
from jax.sharding import PartitionSpec as P

F32 = jnp.float32
BF16 = jnp.bfloat16
CHUNKS = 2
BLOCK = 8
VMEM_LIMIT = 32 * 1024 * 1024
FIRST_LIMIT = 60 * 1024 * 1024


def split(value):
    high = value.astype(BF16)
    return high, (value - high.astype(F32)).astype(BF16)


def product(left, right):
    dot = functools.partial(jnp.dot, preferred_element_type=F32)
    return dot(left[0], right[0]) + (dot(left[0], right[1]) + dot(left[1], right[0]))


def react(value, kinetics):
    rate, level = kinetics
    return value - rate * jnp.tanh(value - level)


def read_kinetics(species_ref, rates_ref, levels_ref):
    index = species_ref[0]
    return rates_ref[index], levels_ref[index]


def relative(index, block, own):
    return ((index // block) ^ own) * block + index % block


def picker(shape, along, source, flag, length):
    wanted = source(lax.broadcasted_iota(jnp.int32, shape, along))
    wanted = jnp.where(flag == 1, length - 1 - wanted, wanted)
    return jnp.where(lax.broadcasted_iota(jnp.int32, shape, 1 - along) == wanted, 1.0, 0.0).astype(BF16)


def combined(inverse, explicit):
    return jnp.dot(inverse, explicit, precision=lax.Precision.HIGHEST, preferred_element_type=F32)


def rearrange(pieces, rows, columns):
    dot = functools.partial(jnp.dot, preferred_element_type=F32)
    return tuple(dot(dot(rows, piece).astype(BF16), columns).astype(BF16) for piece in pieces)


def sending_order(ranks):
    half = ranks // 2
    order = []
    for index in range(half):
        order.append(half + index)
        order += [half - 1 - near for near in range(half - 1) if near - near // 5 == index]
    return order + [0]


def by_place(refs):
    order = sending_order(len(refs))
    return [refs[order.index(place)] for place in range(len(refs))]


def position():
    return lax.axis_index("row"), lax.axis_index("col")


def first_sweep(chunk, columns, species, rates, levels, flags, explicit, inverse, field, *refs):
    blocks = by_place(refs[:-5])
    held, matrices, high, low, done = refs[-5:]
    ranks = len(blocks)
    depth, each, width = blocks[0].shape
    row, column = position()
    own = row * columns + column

    step, steps = pl.program_id(0), held.shape[0]

    def arrival(index):
        part = field.at[:, pl.ds(index * depth, depth), :]
        return pltpu.make_async_copy(part, held.at[index], done.at[index])

    @pl.when(step == 0)
    def _():
        copies = [
            pltpu.make_async_copy(source, matrices.at[index], done.at[steps + index])
            for index, source in enumerate((inverse, explicit))
        ]
        for copy in copies:
            copy.start()
        for index in range(steps):
            arrival(index).start()
        for copy in copies:
            copy.wait()
        share, length = high.shape
        pieces = split(combined(matrices[0], matrices[1]))
        flag = flags[0, 0]
        high[...], low[...] = rearrange(
            pieces,
            picker((share, length), 0, lambda i: chunk * share + relative(i, each, own), flag, length),
            picker((length, length), 1, lambda i: i, flag, length),
        )

    arrival(step).wait()
    kinetics = read_kinetics(species, rates, levels)
    matrix = (high[...], low[...])
    for cell in range(0, depth, 2):
        value = jnp.concatenate([held[step, :, cell, :], held[step, :, cell + 1, :]], axis=1)
        result = product(matrix, split(react(value, kinetics)))
        for half in range(2):
            part = result[:, half * width : (half + 1) * width].reshape(ranks, each, width)
            for place in range(ranks):
                blocks[place][cell + half] = part[place]


def last_sweep(chunk, columns, ranks, species, rates, levels, flags, explicit, inverse, *refs):
    blocks, refs = by_place(refs[:ranks]), refs[ranks:]
    total = refs[0] if chunk > 0 else None
    out, high, low = refs[-3:]
    each, width = blocks[0].shape[1:]
    depth = out.shape[1] if chunk > 0 else out.shape[0]
    first = pl.program_id(0) * depth
    row, column = position()
    own = row * columns + column

    @pl.when(pl.program_id(0) == 0)
    def _():
        length, share = high.shape
        flag = flags[flags.shape[0] - 1, 0]
        pieces = split(combined(inverse[...], explicit[...]))
        high[...], low[...] = rearrange(
            pieces,
            picker((length, length), 0, lambda i: i, flag, length),
            picker((length, share), 1, lambda i: chunk * share + relative(i, each, own), flag, length),
        )

    kinetics = read_kinetics(species, rates, levels)
    matrix = (high[...], low[...])
    for cell in range(0, depth, 2):
        value = jnp.concatenate(
            [
                jnp.concatenate([block[first + cell + half] for block in blocks], axis=0)
                for half in range(2)
            ],
            axis=1,
        )
        result = product(matrix, split(react(value, kinetics)))
        for half in range(2):
            part = result[:, half * width : (half + 1) * width]
            if chunk > 0:
                out[:, cell + half, :] = part + total[first + cell + half]
            else:
                out[cell + half] = part


def prepare(depth, width, flags, explicit_line, inverse_line, explicit_depth, inverse_depth, high, low):
    row, column = position()
    line = split(combined(inverse_line[...], explicit_line[...]))
    deep = split(combined(inverse_depth[...], explicit_depth[...]).T)
    for place, (pieces, step, axis_dim) in enumerate(
        [(line, 0, 1), (deep, 0, 2), (deep, 1, 2), (line, 1, 1)]
    ):
        own, block = (row, depth) if axis_dim == 1 else (column, width)
        shape = pieces[0].shape
        flag = flags[step, axis_dim]
        high[place], low[place] = rearrange(
            pieces,
            *[picker(shape, along, lambda i: relative(i, block, own), flag, shape[0]) for along in range(2)],
        )


def plane_sweeps(columns, species, rates, levels, high, low, *refs):
    ranks = len(refs) // 2
    blocks, outs = by_place(refs[:ranks]), by_place(refs[ranks:])
    depth, each, width = blocks[0].shape
    rows = ranks // columns
    kinetics = read_kinetics(species, rates, levels)
    for cell in range(each):
        value = jnp.concatenate(
            [
                jnp.concatenate([blocks[r * columns + c][:, cell, :] for c in range(columns)], axis=1)
                for r in range(rows)
            ],
            axis=0,
        )
        for place in range(4):
            pieces = split(react(value, kinetics))
            matrix = (high[place], low[place])
            value = product(matrix, pieces) if place in (0, 3) else product(pieces, matrix)
        for place in range(ranks):
            r, c = place // columns, place % columns
            outs[place][:, cell, :] = value[r * depth : (r + 1) * depth, c * width : (c + 1) * width]


PARAMS = pltpu.CompilerParams(vmem_limit_bytes=VMEM_LIMIT)
VMEM = pl.BlockSpec(memory_space=pltpu.VMEM)


def scalars(shape):
    return pl.BlockSpec(shape, lambda i: (0,) * len(shape), memory_space=pltpu.SMEM)


def whole(shape):
    return pl.BlockSpec(shape, lambda i: (0,) * len(shape))


def cost(cells, length, sweeps, bytes_accessed):
    return pl.CostEstimate(
        flops=6 * cells * length * sweeps, bytes_accessed=bytes_accessed, transcendentals=cells * sweeps
    )


def fast(rows, columns, concentration, species, reaction_rates, levels, sweep_flags,
         explicit_line, inverse_line, explicit_depth, inverse_depth):
    lines, depth, width = concentration.shape
    ranks = rows * columns
    share = lines // CHUNKS
    each = share // ranks
    size = lines * depth * width
    kinetic = (species, reaction_rates, levels)
    kinetic_specs = [scalars(array.shape) for array in kinetic]
    flags_spec = scalars(sweep_flags.shape)
    matrix_spec = whole((lines, lines))
    home_spec = pl.BlockSpec((lines, BLOCK, width), lambda i: (0, i, 0))
    chunk_shapes = [jax.ShapeDtypeStruct((depth, each, width), F32)] * ranks
    depth_specs = [pl.BlockSpec((BLOCK, each, width), lambda i: (i, 0, 0))] * ranks
    plane_specs = [VMEM] * ranks

    def exchange(blocks):
        return [
            lax.ppermute(block, ("row", "col"), [(i, i ^ place) for i in range(ranks)]) if place else block
            for place, block in zip(sending_order(ranks), blocks)
        ]

    def first(chunk):
        return pl.pallas_call(
            functools.partial(first_sweep, chunk, columns),
            grid=(depth // BLOCK,),
            in_specs=kinetic_specs + [flags_spec] + [pl.BlockSpec(memory_space=pl.ANY)] * 3,
            out_specs=depth_specs,
            out_shape=chunk_shapes,
            scratch_shapes=[
                pltpu.VMEM((depth // BLOCK, lines, BLOCK, width), F32),
                pltpu.VMEM((2, lines, lines), F32),
                pltpu.VMEM((share, lines), BF16),
                pltpu.VMEM((share, lines), BF16),
                pltpu.SemaphoreType.DMA((depth // BLOCK + 2,)),
            ],
            compiler_params=pltpu.CompilerParams(vmem_limit_bytes=FIRST_LIMIT),
            cost_estimate=cost(size // CHUNKS, lines, 1, 4 * (size + size // CHUNKS)),
            name=f"first_sweep_{chunk}",
        )(*kinetic, sweep_flags, explicit_line, inverse_line, concentration)

    def planes(blocks, chunk):
        return pl.pallas_call(
            functools.partial(plane_sweeps, columns),
            grid=(1,),
            in_specs=kinetic_specs + [whole((4, lines, lines))] * 2 + plane_specs,
            out_specs=plane_specs,
            out_shape=chunk_shapes,
            compiler_params=PARAMS,
            cost_estimate=cost(size // CHUNKS, lines, 4, 8 * size // CHUNKS),
            name=f"plane_sweeps_{chunk}",
        )(*kinetic, high, low, *blocks)

    def last(blocks, total, chunk):
        more = [] if chunk == 0 else [total]
        return pl.pallas_call(
            functools.partial(last_sweep, chunk, columns, ranks),
            grid=(depth // BLOCK,),
            in_specs=kinetic_specs + [flags_spec] + [matrix_spec] * 2 + [VMEM] * ranks + [VMEM] * len(more),
            out_specs=home_spec if more else pl.BlockSpec((BLOCK, lines, width), lambda i: (i, 0, 0)),
            out_shape=jax.ShapeDtypeStruct((lines, depth, width) if more else (depth, lines, width), F32),
            scratch_shapes=[pltpu.VMEM((lines, share), BF16)] * 2,
            compiler_params=PARAMS,
            cost_estimate=cost(size // CHUNKS, lines, 1, 4 * (size + size // CHUNKS)),
            name=f"last_sweep_{chunk}",
        )(*kinetic, sweep_flags, explicit_line, inverse_line, *blocks, *more)

    pieces_shape = jax.ShapeDtypeStruct((4, lines, lines), BF16)
    high, low = pl.pallas_call(
        functools.partial(prepare, depth, width),
        grid=(1,),
        in_specs=[flags_spec] + [matrix_spec] * 4,
        out_specs=[whole((4, lines, lines))] * 2,
        out_shape=[pieces_shape] * 2,
        compiler_params=PARAMS,
        cost_estimate=cost(lines * lines, lines, 8, 8 * 4 * lines * lines),
        name="prepare",
    )(sweep_flags, explicit_line, inverse_line, explicit_depth, inverse_depth)

    there = [exchange(first(chunk)) for chunk in range(CHUNKS)]
    back = [exchange(planes(there[chunk], chunk)) for chunk in range(CHUNKS)]
    total = None
    for chunk in range(CHUNKS):
        total = last(back[chunk], total, chunk)
    return total


def oriented(matrix, reflect):
    return jnp.where(reflect == 1, matrix[::-1, ::-1], matrix)


def plain(concentration, species, reaction_rates, levels, sweep_flags,
          explicit_line, inverse_line, explicit_depth, inverse_depth):
    kinetics = (reaction_rates[species[0]], levels[species[0]])
    matmul = functools.partial(jnp.einsum, precision=lax.Precision.HIGHEST)
    line = matmul("ij,jk->ik", inverse_line, explicit_line)
    deep = matmul("ij,jk->ik", inverse_depth, explicit_depth)
    letters = ["ij,jbc->ibc", "ij,ajc->aic", "ij,abj->abi"]

    def sweep(value, step, axis_dim):
        matrix = oriented(deep if axis_dim == 2 else line, sweep_flags[step, axis_dim])
        return matmul(letters[axis_dim], matrix, react(value, kinetics))

    def regroup(value):
        value = lax.all_to_all(value, "row", split_axis=0, concat_axis=1, tiled=True)
        return lax.all_to_all(value, "col", split_axis=0, concat_axis=2, tiled=True)

    def restore(value):
        value = lax.all_to_all(value, "col", split_axis=2, concat_axis=0, tiled=True)
        return lax.all_to_all(value, "row", split_axis=1, concat_axis=0, tiled=True)

    value, home = concentration, True
    for step in range(sweep_flags.shape[0]):
        for axis_dim in [0, 1, 2] if step % 2 == 0 else [2, 1, 0]:
            if home != (axis_dim == 0):
                value = restore(value) if axis_dim == 0 else regroup(value)
                home = axis_dim == 0
            value = sweep(value, step, axis_dim)
    return value if home else restore(value)


def solution(mesh):
    rows, columns = mesh.shape["row"], mesh.shape["col"]
    ranks = rows * columns

    def on_device(*args):
        lines, depth, width = args[0].shape
        fits = (
            args[4].shape[0] == 2
            and ranks & (ranks - 1) == 0
            and ranks >= 2
            and lines % (ranks * CHUNKS * 8) == 0
            and depth % BLOCK == 0
            and width % 128 == 0
            and depth * rows == lines
            and width * columns == args[7].shape[0] == lines
        )
        if fits:
            return fast(rows, columns, *args)
        return plain(*args)

    in_specs = (P("groups", "row", "col"), P("groups"), P(), P(), P(), P(), P(), P(), P())
    return jax.shard_map(
        on_device, mesh=mesh, in_specs=in_specs, out_specs=P("groups", "row", "col"), check_vma=False
    )
```

```python
import functools
import jax
import jax.numpy as jnp
from jax import lax
from jax.experimental import pallas as pl
from jax.experimental.pallas import tpu as pltpu
from jax.sharding import PartitionSpec as P

F32 = jnp.float32
BF16 = jnp.bfloat16
CHUNKS = 2
BLOCK = 8
VMEM_LIMIT = 24 * 1024 * 1024
FIRST_LIMIT = 60 * 1024 * 1024
GRAIN = 16
OUT_GRAIN = 4
LATE = 5


def split(value):
    high = value.astype(BF16)
    return high, (value - high.astype(F32)).astype(BF16)


def product(left, right):
    dot = functools.partial(jnp.dot, preferred_element_type=F32)
    rows = left[0].shape[0]
    both = dot(jnp.concatenate(left, axis=0), right[0])
    return both[:rows] + (both[rows:] + dot(left[0], right[1]))


def react(value, kinetics):
    rate, level = kinetics
    return value - rate * jnp.tanh(value - level)


def read_kinetics(species_ref, rates_ref, levels_ref):
    index = species_ref[0]
    return rates_ref[index], levels_ref[index]


def relative(index, block, own):
    return ((index // block) ^ own) * block + index % block


def picker(shape, along, source, flag, length):
    wanted = source(lax.broadcasted_iota(jnp.int32, shape, along))
    wanted = jnp.where(flag == 1, length - 1 - wanted, wanted)
    return jnp.where(lax.broadcasted_iota(jnp.int32, shape, 1 - along) == wanted, 1.0, 0.0).astype(BF16)


def combined(inverse, explicit):
    return jnp.dot(inverse, explicit, precision=lax.Precision.HIGHEST, preferred_element_type=F32)


def rearrange(pieces, rows, columns):
    dot = functools.partial(jnp.dot, preferred_element_type=F32)
    return tuple(dot(dot(rows, piece).astype(BF16), columns).astype(BF16) for piece in pieces)


def sending_order(ranks):
    half = ranks // 2
    order = []
    for index in range(half):
        order.append(half + index)
        order += [half - 1 - near for near in range(half - 1) if near - near // 5 == index]
    return order + [0]


def arrivals(ranks):
    order = sending_order(ranks)
    late = order[-1 - LATE : -1]
    early = [(chunk, place) for chunk in range(CHUNKS - 1) for place in order]
    early += [(CHUNKS - 1, place) for place in order if place not in late]
    return early, [(CHUNKS - 1, place) for place in late]


def by_place(refs):
    order = sending_order(len(refs))
    return [refs[order.index(place)] for place in range(len(refs))]


def position():
    return lax.axis_index("row"), lax.axis_index("col")


def first_sweep(chunk, columns, species, rates, levels, flags, explicit, inverse, field, *refs):
    blocks = by_place(refs[:-7])
    held, matrices, done, *small = refs[-7:]
    ranks = len(blocks)
    depth, each, width = blocks[0].shape
    length = field.shape[0]
    row, column = position()
    own = row * columns + column
    targets = [*small, matrices.at[0], matrices.at[1]] + [held.at[cell] for cell in range(depth)]
    sources = [species, rates, levels, flags, inverse, explicit]
    sources += [field.at[:, cell, :] for cell in range(depth)]
    copies = [
        pltpu.make_async_copy(source, target, done.at[index])
        for index, (source, target) in enumerate(zip(sources, targets))
    ]
    for copy in copies:
        copy.start()
    for copy in copies[:-depth]:
        copy.wait()
    species, rates, levels, flags = small
    share = ranks * each
    flag = flags[0, 0]
    matrix = rearrange(
        split(combined(matrices[0], matrices[1])),
        picker((share, length), 0, lambda i: chunk * share + relative(i, each, own), flag, length),
        picker((length, length), 1, lambda i: i, flag, length),
    )
    kinetics = read_kinetics(species, rates, levels)
    for cell in range(0, depth, 2):
        if cell % GRAIN == 0:
            for copy in copies[len(copies) - depth + cell :][:GRAIN]:
                copy.wait()
        value = jnp.concatenate([held[cell], held[cell + 1]], axis=1)
        result = product(matrix, split(react(value, kinetics)))
        for half in range(2):
            piece = result[:, half * width : (half + 1) * width].reshape(ranks, each, width)
            for place in range(ranks):
                blocks[place][cell + half] = piece[place]


def block_sums(blocks, cell, matrix, kinetics):
    value = jnp.concatenate(
        [jnp.concatenate([block[cell + half] for block in blocks], axis=0) for half in range(2)], axis=1
    )
    return product(matrix, split(react(value, kinetics)))


def partial_sums(kinetics, high, low, *refs):
    blocks, out = refs[:-1], refs[-1]
    depth, _, width = out.shape
    for cell in range(0, depth, 2):
        index = pl.program_id(0) * depth + cell
        result = block_sums(blocks, index, (high[...], low[...]), (kinetics[0:1, :], kinetics[1:2, :]))
        out[cell] = result[:, :width]
        out[cell + 1] = result[:, width:]


def last_sweep(kinetics, high, low, *refs):
    blocks, (total, out, held, done) = refs[:-4], refs[-4:]
    depth, _, width = held.shape
    copies = [
        pltpu.make_async_copy(held.at[cell], out.at[:, cell, :], done.at[cell]) for cell in range(depth)
    ]
    for cell in range(0, depth, 2):
        result = block_sums(blocks, cell, (high[...], low[...]), (kinetics[0:1, :], kinetics[1:2, :]))
        held[cell] = result[:, :width] + total[cell]
        held[cell + 1] = result[:, width:] + total[cell + 1]
        if (cell + 2) % OUT_GRAIN == 0:
            for copy in copies[cell + 2 - OUT_GRAIN : cell + 2]:
                copy.start()
    for copy in copies:
        copy.wait()


def prepare(columns, depth, width, each, species, rates, levels, flags, explicit_line, inverse_line,
            explicit_depth, inverse_depth, kinetics, high, low, *last):
    row, column = position()
    rate, level = read_kinetics(species, rates, levels)
    kinetics[0:1, :] = jnp.full((1, kinetics.shape[1]), rate, F32)
    kinetics[1:2, :] = jnp.full((1, kinetics.shape[1]), level, F32)
    line = split(combined(inverse_line[...], explicit_line[...]))
    deep = split(combined(inverse_depth[...], explicit_depth[...]).T)
    shape = line[0].shape
    for place, (pieces, step, axis_dim) in enumerate(
        [(line, 0, 1), (deep, 0, 2), (deep, 1, 2), (line, 1, 1)]
    ):
        own, block = (row, depth) if axis_dim == 1 else (column, width)
        flag = flags[step, axis_dim]
        high[place], low[place] = rearrange(
            pieces,
            *[picker(shape, along, lambda i: relative(i, block, own), flag, shape[0]) for along in range(2)],
        )
    own = row * columns + column
    rows = picker(shape, 0, lambda i: i, flags[1, 0], shape[0])
    for blocks, high, low in zip(arrivals(shape[0] // CHUNKS // each), last[0::2], last[1::2]):

        def source(index):
            cell = index % each
            for number, (chunk, place) in enumerate(blocks):
                start = chunk * (shape[0] // CHUNKS) + (place ^ own) * each
                cell = jnp.where(index // each == number, start + index % each, cell)
            return cell

        selected = (shape[0], len(blocks) * each)
        high[...], low[...] = rearrange(line, rows, picker(selected, 1, source, flags[1, 0], shape[0]))


def plane_sweeps(columns, ranks, kinetics, high, low, *refs):
    refs, field = refs[:-1], refs[-1]
    groups = [by_place(refs[i : i + ranks]) for i in range(0, len(refs), ranks)]
    depths = [group[0].shape[0] for group in groups]
    _, each, width = groups[0][0].shape
    rows = ranks // columns
    depth = high.shape[1] // rows
    splits = next(i for i in range(len(groups)) if sum(depths[:i]) == depth)
    ins, outs = groups[:splits], groups[splits:]
    rate_level = (kinetics[0:1, :], kinetics[1:2, :])
    for place in range(ranks):
        start = place // columns * depth
        lanes = slice(place % columns * width, (place % columns + 1) * width)
        for group in ins:
            for line in range(0, group[place].shape[0], BLOCK):
                field[:, start + line : start + line + BLOCK, lanes] = jnp.swapaxes(
                    group[place][line : line + BLOCK], 0, 1
                )
            start += group[place].shape[0]
    for cell in range(each):
        value = field[cell]
        for place in range(4):
            pieces = split(react(value, rate_level))
            matrix = (high[place], low[place])
            value = product(matrix, pieces) if place in (0, 3) else product(pieces, matrix)
        field[cell] = value
    for place in range(ranks):
        start = place // columns * depth
        lanes = slice(place % columns * width, (place % columns + 1) * width)
        for group in outs:
            for line in range(0, group[place].shape[0], BLOCK):
                group[place][line : line + BLOCK] = jnp.swapaxes(
                    field[:, start + line : start + line + BLOCK, lanes], 0, 1
                )
            start += group[place].shape[0]


PARAMS = pltpu.CompilerParams(vmem_limit_bytes=VMEM_LIMIT)
VMEM = pl.BlockSpec(memory_space=pltpu.VMEM)
HBM = pl.BlockSpec(memory_space=pltpu.HBM)


def scalars(shape):
    return pl.BlockSpec(shape, lambda i: (0,) * len(shape), memory_space=pltpu.SMEM)


def whole(shape):
    return pl.BlockSpec(shape, lambda i: (0,) * len(shape))


def cost(cells, length, sweeps, bytes_accessed):
    return pl.CostEstimate(
        flops=6 * cells * length * sweeps, bytes_accessed=bytes_accessed, transcendentals=cells * sweeps
    )


def fast(rows, columns, concentration, species, reaction_rates, levels, sweep_flags,
         explicit_line, inverse_line, explicit_depth, inverse_depth):
    lines, depth, width = concentration.shape
    ranks = rows * columns
    share = lines // CHUNKS
    each = share // ranks
    size = lines * depth * width
    scalar_arrays = (species, reaction_rates, levels, sweep_flags)
    scalar_specs = [scalars(array.shape) for array in scalar_arrays]
    order = sending_order(ranks)

    def exchange(blocks):
        return [
            lax.ppermute(block, ("row", "col"), [(i, i ^ place) for i in range(ranks)]) if place else block
            for place, block in zip(order, blocks)
        ]

    def block_shapes(count):
        return [jax.ShapeDtypeStruct((count, each, width), F32)] * ranks

    def first(chunk):
        return pl.pallas_call(
            functools.partial(first_sweep, chunk, columns),
            grid=(1,),
            in_specs=[HBM] * 7,
            out_specs=[VMEM] * ranks,
            out_shape=block_shapes(depth),
            scratch_shapes=[
                pltpu.VMEM((depth, lines, width), F32),
                pltpu.VMEM((2, lines, lines), F32),
                pltpu.SemaphoreType.DMA((depth + 2 + len(scalar_arrays),)),
                *[pltpu.SMEM(array.shape, array.dtype) for array in scalar_arrays],
            ],
            compiler_params=PARAMS if chunk else pltpu.CompilerParams(vmem_limit_bytes=FIRST_LIMIT),
            cost_estimate=cost(size // CHUNKS, lines, 1, 4 * (size + size // CHUNKS)),
            name=f"first_sweep_{chunk}",
        )(*scalar_arrays, explicit_line, inverse_line, concentration)

    def planes(pieces, chunk, parts):
        outs = pl.pallas_call(
            functools.partial(plane_sweeps, columns, ranks),
            grid=(1,),
            in_specs=[VMEM] * (3 + ranks * len(pieces)),
            out_specs=[VMEM] * (ranks * len(parts)),
            out_shape=[shape for _, count in parts for shape in block_shapes(count)],
            scratch_shapes=[pltpu.VMEM((each, lines, lines), F32)],
            compiler_params=PARAMS,
            cost_estimate=cost(size // CHUNKS, lines, 4, 8 * size // CHUNKS),
            name=f"plane_sweeps_{chunk}",
        )(kinetics, high, low, *[block for blocks in pieces for block in blocks])
        return [outs[i * ranks : (i + 1) * ranks] for i in range(len(parts))]

    def early_sums(blocks, matrix):
        return pl.pallas_call(
            partial_sums,
            grid=(depth // BLOCK,),
            in_specs=[VMEM] * (3 + len(blocks)),
            out_specs=pl.BlockSpec((BLOCK, lines, width), lambda i: (i, 0, 0)),
            out_shape=jax.ShapeDtypeStruct((depth, lines, width), F32),
            compiler_params=PARAMS,
            cost_estimate=cost(size // CHUNKS, lines, 1, 4 * (size + size // CHUNKS)),
            name="partial_sums",
        )(kinetics, *matrix, *blocks)

    def last(blocks, matrix, total):
        return pl.pallas_call(
            last_sweep,
            grid=(1,),
            in_specs=[VMEM] * (4 + len(blocks)),
            out_specs=HBM,
            out_shape=jax.ShapeDtypeStruct((lines, depth, width), F32),
            scratch_shapes=[pltpu.VMEM((depth, lines, width), F32), pltpu.SemaphoreType.DMA((depth,))],
            compiler_params=PARAMS,
            cost_estimate=cost(size // CHUNKS, lines, 1, 4 * (size + size // CHUNKS)),
            name="last_sweep",
        )(kinetics, *matrix, *blocks, total)

    matrix_spec = whole((lines, lines))
    outputs = [
        jax.ShapeDtypeStruct((2, 2 * width), F32),
        *[jax.ShapeDtypeStruct((4, lines, lines), BF16)] * 2,
        *[
            jax.ShapeDtypeStruct((lines, len(blocks) * each), BF16)
            for blocks in arrivals(ranks)
            for _ in range(2)
        ],
    ]
    kinetics, high, low, *last_matrices = pl.pallas_call(
        functools.partial(prepare, columns, depth, width, each),
        grid=(1,),
        in_specs=scalar_specs + [matrix_spec] * 4,
        out_specs=[whole(output.shape) for output in outputs],
        out_shape=outputs,
        compiler_params=PARAMS,
        cost_estimate=cost(lines * lines, lines, 8, 8 * 4 * lines * lines),
        name="prepare",
    )(*scalar_arrays, explicit_line, inverse_line, explicit_depth, inverse_depth)

    there = [exchange(first(chunk)) for chunk in range(CHUNKS)]
    back = [exchange(planes([there[chunk]], chunk, [(0, depth)])[0]) for chunk in range(CHUNKS)]
    early, late = [
        [back[chunk][order.index(place)] for chunk, place in blocks] for blocks in arrivals(ranks)
    ]
    return last(late, last_matrices[2:], early_sums(early, last_matrices[:2]))


def oriented(matrix, reflect):
    return jnp.where(reflect == 1, matrix[::-1, ::-1], matrix)


def plain(concentration, species, reaction_rates, levels, sweep_flags,
          explicit_line, inverse_line, explicit_depth, inverse_depth):
    kinetics = (reaction_rates[species[0]], levels[species[0]])
    matmul = functools.partial(jnp.einsum, precision=lax.Precision.HIGHEST)
    line = matmul("ij,jk->ik", inverse_line, explicit_line)
    deep = matmul("ij,jk->ik", inverse_depth, explicit_depth)
    letters = ["ij,jbc->ibc", "ij,ajc->aic", "ij,abj->abi"]

    def sweep(value, step, axis_dim):
        matrix = oriented(deep if axis_dim == 2 else line, sweep_flags[step, axis_dim])
        return matmul(letters[axis_dim], matrix, react(value, kinetics))

    def regroup(value):
        value = lax.all_to_all(value, "row", split_axis=0, concat_axis=1, tiled=True)
        return lax.all_to_all(value, "col", split_axis=0, concat_axis=2, tiled=True)

    def restore(value):
        value = lax.all_to_all(value, "col", split_axis=2, concat_axis=0, tiled=True)
        return lax.all_to_all(value, "row", split_axis=1, concat_axis=0, tiled=True)

    value, home = concentration, True
    for step in range(sweep_flags.shape[0]):
        for axis_dim in [0, 1, 2] if step % 2 == 0 else [2, 1, 0]:
            if home != (axis_dim == 0):
                value = restore(value) if axis_dim == 0 else regroup(value)
                home = axis_dim == 0
            value = sweep(value, step, axis_dim)
    return value if home else restore(value)


def solution(mesh):
    rows, columns = mesh.shape["row"], mesh.shape["col"]
    ranks = rows * columns

    def on_device(*args):
        lines, depth, width = args[0].shape
        fits = (
            args[4].shape[0] == 2
            and ranks & (ranks - 1) == 0
            and ranks >= 2
            and lines % (ranks * CHUNKS * 8) == 0
            and depth % BLOCK == 0
            and width % 128 == 0
            and depth * rows == lines
            and width * columns == args[7].shape[0] == lines
            and 2 * width == lines
        )
        if fits:
            return fast(rows, columns, *args)
        return plain(*args)

    in_specs = (P("groups", "row", "col"), P("groups"), P(), P(), P(), P(), P(), P(), P())
    return jax.shard_map(
        on_device, mesh=mesh, in_specs=in_specs, out_specs=P("groups", "row", "col"), check_vma=False
    )
```

```python
import functools
import jax
import jax.numpy as jnp
from jax import lax
from jax.experimental import pallas as pl
from jax.experimental.pallas import tpu as pltpu
from jax.sharding import PartitionSpec as P

F32 = jnp.float32
BF16 = jnp.bfloat16
CHUNKS = 2
BLOCK = 8
VMEM_LIMIT = 24 * 1024 * 1024
FIRST_LIMIT = 60 * 1024 * 1024
GRAIN = 16
OUT_GRAIN = 4
LATE = 5


def split(value):
    high = value.astype(BF16)
    return high, (value - high.astype(F32)).astype(BF16)


def product(left, right):
    dot = functools.partial(jnp.dot, preferred_element_type=F32)
    rows = left[0].shape[0]
    both = dot(jnp.concatenate(left, axis=0), right[0])
    return both[:rows] + (both[rows:] + dot(left[0], right[1]))


def react(value, kinetics):
    rate, level = kinetics
    return value - rate * jnp.tanh(value - level)


def read_kinetics(species_ref, rates_ref, levels_ref):
    index = species_ref[0]
    return rates_ref[index], levels_ref[index]


def relative(index, block, own):
    return ((index // block) ^ own) * block + index % block


def picker(shape, along, source, flag, length):
    wanted = source(lax.broadcasted_iota(jnp.int32, shape, along))
    wanted = jnp.where(flag == 1, length - 1 - wanted, wanted)
    return jnp.where(lax.broadcasted_iota(jnp.int32, shape, 1 - along) == wanted, 1.0, 0.0).astype(BF16)


def combined(inverse, explicit):
    return jnp.dot(inverse, explicit, precision=lax.Precision.HIGHEST, preferred_element_type=F32)


def rearrange(pieces, rows, columns):
    dot = functools.partial(jnp.dot, preferred_element_type=F32)
    return tuple(dot(dot(rows, piece).astype(BF16), columns).astype(BF16) for piece in pieces)


def sending_order(ranks):
    half = ranks // 2
    order = []
    for index in range(half):
        order.append(half + (index ^ (index >> 1) if 2 * index < half else 3 * half // 2 - 1 - index))
        order += [half - 1 - near for near in range(half - 1) if near - near // 5 == index]
    return order + [0]


def arrivals(ranks):
    order = sending_order(ranks)
    late = order[-1 - LATE : -1]
    early = [(chunk, place) for chunk in range(CHUNKS - 1) for place in order]
    early += [(CHUNKS - 1, place) for place in order if place not in late]
    return early, [(CHUNKS - 1, place) for place in late]


def by_place(refs):
    order = sending_order(len(refs))
    return [refs[order.index(place)] for place in range(len(refs))]


def position():
    return lax.axis_index("row"), lax.axis_index("col")


def first_sweep(chunk, columns, species, rates, levels, flags, explicit, inverse, field, *refs):
    blocks = by_place(refs[:-7])
    held, matrices, done, *small = refs[-7:]
    ranks = len(blocks)
    depth, each, width = blocks[0].shape
    length = field.shape[0]
    row, column = position()
    own = row * columns + column
    targets = [*small, matrices.at[0], matrices.at[1]] + [held.at[cell] for cell in range(depth)]
    sources = [species, rates, levels, flags, inverse, explicit]
    sources += [field.at[:, cell, :] for cell in range(depth)]
    copies = [
        pltpu.make_async_copy(source, target, done.at[index])
        for index, (source, target) in enumerate(zip(sources, targets))
    ]
    for copy in copies:
        copy.start()
    for copy in copies[:-depth]:
        copy.wait()
    species, rates, levels, flags = small
    share = ranks * each
    flag = flags[0, 0]
    matrix = rearrange(
        split(combined(matrices[0], matrices[1])),
        picker((share, length), 0, lambda i: chunk * share + relative(i, each, own), flag, length),
        picker((length, length), 1, lambda i: i, flag, length),
    )
    kinetics = read_kinetics(species, rates, levels)
    for cell in range(0, depth, 2):
        if cell % GRAIN == 0:
            for copy in copies[len(copies) - depth + cell :][:GRAIN]:
                copy.wait()
        value = jnp.concatenate([held[cell], held[cell + 1]], axis=1)
        result = product(matrix, split(react(value, kinetics)))
        for half in range(2):
            piece = result[:, half * width : (half + 1) * width].reshape(ranks, each, width)
            for place in range(ranks):
                blocks[place][cell + half] = piece[place]


def block_sums(blocks, cell, matrix, kinetics):
    value = jnp.concatenate(
        [jnp.concatenate([block[cell + half] for block in blocks], axis=0) for half in range(2)], axis=1
    )
    return product(matrix, split(react(value, kinetics)))


def partial_sums(kinetics, high, low, *refs):
    blocks, out = refs[:-1], refs[-1]
    depth, _, width = out.shape
    for cell in range(0, depth, 2):
        index = pl.program_id(0) * depth + cell
        result = block_sums(blocks, index, (high[...], low[...]), (kinetics[0:1, :], kinetics[1:2, :]))
        out[cell] = result[:, :width]
        out[cell + 1] = result[:, width:]


def last_sweep(kinetics, high, low, *refs):
    blocks, (total, out, held, done) = refs[:-4], refs[-4:]
    depth, _, width = held.shape
    copies = [
        pltpu.make_async_copy(held.at[cell], out.at[:, cell, :], done.at[cell]) for cell in range(depth)
    ]
    for cell in range(0, depth, 2):
        result = block_sums(blocks, cell, (high[...], low[...]), (kinetics[0:1, :], kinetics[1:2, :]))
        held[cell] = result[:, :width] + total[cell]
        held[cell + 1] = result[:, width:] + total[cell + 1]
        if (cell + 2) % OUT_GRAIN == 0:
            for copy in copies[cell + 2 - OUT_GRAIN : cell + 2]:
                copy.start()
    for copy in copies:
        copy.wait()


def prepare(columns, depth, width, each, species, rates, levels, flags, explicit_line, inverse_line,
            explicit_depth, inverse_depth, kinetics, high, low, *last):
    row, column = position()
    rate, level = read_kinetics(species, rates, levels)
    kinetics[0:1, :] = jnp.full((1, kinetics.shape[1]), rate, F32)
    kinetics[1:2, :] = jnp.full((1, kinetics.shape[1]), level, F32)
    line = split(combined(inverse_line[...], explicit_line[...]))
    deep = split(combined(inverse_depth[...], explicit_depth[...]).T)
    shape = line[0].shape
    for place, (pieces, step, axis_dim) in enumerate(
        [(line, 0, 1), (deep, 0, 2), (deep, 1, 2), (line, 1, 1)]
    ):
        own, block = (row, depth) if axis_dim == 1 else (column, width)
        flag = flags[step, axis_dim]
        high[place], low[place] = rearrange(
            pieces,
            *[picker(shape, along, lambda i: relative(i, block, own), flag, shape[0]) for along in range(2)],
        )
    own = row * columns + column
    rows = picker(shape, 0, lambda i: i, flags[1, 0], shape[0])
    for blocks, high, low in zip(arrivals(shape[0] // CHUNKS // each), last[0::2], last[1::2]):

        def source(index):
            cell = index % each
            for number, (chunk, place) in enumerate(blocks):
                start = chunk * (shape[0] // CHUNKS) + (place ^ own) * each
                cell = jnp.where(index // each == number, start + index % each, cell)
            return cell

        selected = (shape[0], len(blocks) * each)
        high[...], low[...] = rearrange(line, rows, picker(selected, 1, source, flags[1, 0], shape[0]))


def plane_sweeps(columns, ranks, kinetics, high, low, *refs):
    refs, field = refs[:-1], refs[-1]
    groups = [by_place(refs[i : i + ranks]) for i in range(0, len(refs), ranks)]
    depths = [group[0].shape[0] for group in groups]
    _, each, width = groups[0][0].shape
    rows = ranks // columns
    depth = high.shape[1] // rows
    splits = next(i for i in range(len(groups)) if sum(depths[:i]) == depth)
    ins, outs = groups[:splits], groups[splits:]
    rate_level = (kinetics[0:1, :], kinetics[1:2, :])
    for place in range(ranks):
        start = place // columns * depth
        lanes = slice(place % columns * width, (place % columns + 1) * width)
        for group in ins:
            for line in range(0, group[place].shape[0], BLOCK):
                field[:, start + line : start + line + BLOCK, lanes] = jnp.swapaxes(
                    group[place][line : line + BLOCK], 0, 1
                )
            start += group[place].shape[0]
    for cell in range(each):
        value = field[cell]
        for place in range(4):
            pieces = split(react(value, rate_level))
            matrix = (high[place], low[place])
            value = product(matrix, pieces) if place in (0, 3) else product(pieces, matrix)
        field[cell] = value
    for place in range(ranks):
        start = place // columns * depth
        lanes = slice(place % columns * width, (place % columns + 1) * width)
        for group in outs:
            for line in range(0, group[place].shape[0], BLOCK):
                group[place][line : line + BLOCK] = jnp.swapaxes(
                    field[:, start + line : start + line + BLOCK, lanes], 0, 1
                )
            start += group[place].shape[0]


PARAMS = pltpu.CompilerParams(vmem_limit_bytes=VMEM_LIMIT)
VMEM = pl.BlockSpec(memory_space=pltpu.VMEM)
HBM = pl.BlockSpec(memory_space=pltpu.HBM)


def scalars(shape):
    return pl.BlockSpec(shape, lambda i: (0,) * len(shape), memory_space=pltpu.SMEM)


def whole(shape):
    return pl.BlockSpec(shape, lambda i: (0,) * len(shape))


def cost(cells, length, sweeps, bytes_accessed):
    return pl.CostEstimate(
        flops=6 * cells * length * sweeps, bytes_accessed=bytes_accessed, transcendentals=cells * sweeps
    )


def fast(rows, columns, concentration, species, reaction_rates, levels, sweep_flags,
         explicit_line, inverse_line, explicit_depth, inverse_depth):
    lines, depth, width = concentration.shape
    ranks = rows * columns
    share = lines // CHUNKS
    each = share // ranks
    size = lines * depth * width
    scalar_arrays = (species, reaction_rates, levels, sweep_flags)
    scalar_specs = [scalars(array.shape) for array in scalar_arrays]
    order = sending_order(ranks)

    def exchange(blocks):
        return [
            lax.ppermute(block, ("row", "col"), [(i, i ^ place) for i in range(ranks)]) if place else block
            for place, block in zip(order, blocks)
        ]

    def block_shapes(count):
        return [jax.ShapeDtypeStruct((count, each, width), F32)] * ranks

    def first(chunk):
        return pl.pallas_call(
            functools.partial(first_sweep, chunk, columns),
            grid=(1,),
            in_specs=[HBM] * 7,
            out_specs=[VMEM] * ranks,
            out_shape=block_shapes(depth),
            scratch_shapes=[
                pltpu.VMEM((depth, lines, width), F32),
                pltpu.VMEM((2, lines, lines), F32),
                pltpu.SemaphoreType.DMA((depth + 2 + len(scalar_arrays),)),
                *[pltpu.SMEM(array.shape, array.dtype) for array in scalar_arrays],
            ],
            compiler_params=pltpu.CompilerParams(vmem_limit_bytes=FIRST_LIMIT),
            cost_estimate=cost(size // CHUNKS, lines, 1, 4 * (size + size // CHUNKS)),
            name=f"first_sweep_{chunk}",
        )(*scalar_arrays, explicit_line, inverse_line, concentration)

    def planes(pieces, chunk, parts):
        outs = pl.pallas_call(
            functools.partial(plane_sweeps, columns, ranks),
            grid=(1,),
            in_specs=[VMEM] * (3 + ranks * len(pieces)),
            out_specs=[VMEM] * (ranks * len(parts)),
            out_shape=[shape for _, count in parts for shape in block_shapes(count)],
            scratch_shapes=[pltpu.VMEM((each, lines, lines), F32)],
            compiler_params=PARAMS,
            cost_estimate=cost(size // CHUNKS, lines, 4, 8 * size // CHUNKS),
            name=f"plane_sweeps_{chunk}",
        )(kinetics, high, low, *[block for blocks in pieces for block in blocks])
        return [outs[i * ranks : (i + 1) * ranks] for i in range(len(parts))]

    def early_sums(blocks, matrix):
        return pl.pallas_call(
            partial_sums,
            grid=(depth // BLOCK,),
            in_specs=[VMEM] * (3 + len(blocks)),
            out_specs=pl.BlockSpec((BLOCK, lines, width), lambda i: (i, 0, 0)),
            out_shape=jax.ShapeDtypeStruct((depth, lines, width), F32),
            compiler_params=PARAMS,
            cost_estimate=cost(size // CHUNKS, lines, 1, 4 * (size + size // CHUNKS)),
            name="partial_sums",
        )(kinetics, *matrix, *blocks)

    def last(blocks, matrix, total):
        return pl.pallas_call(
            last_sweep,
            grid=(1,),
            in_specs=[VMEM] * (4 + len(blocks)),
            out_specs=HBM,
            out_shape=jax.ShapeDtypeStruct((lines, depth, width), F32),
            scratch_shapes=[pltpu.VMEM((depth, lines, width), F32), pltpu.SemaphoreType.DMA((depth,))],
            compiler_params=PARAMS,
            cost_estimate=cost(size // CHUNKS, lines, 1, 4 * (size + size // CHUNKS)),
            name="last_sweep",
        )(kinetics, *matrix, *blocks, total)

    matrix_spec = whole((lines, lines))
    outputs = [
        jax.ShapeDtypeStruct((2, 2 * width), F32),
        *[jax.ShapeDtypeStruct((4, lines, lines), BF16)] * 2,
        *[
            jax.ShapeDtypeStruct((lines, len(blocks) * each), BF16)
            for blocks in arrivals(ranks)
            for _ in range(2)
        ],
    ]
    kinetics, high, low, *last_matrices = pl.pallas_call(
        functools.partial(prepare, columns, depth, width, each),
        grid=(1,),
        in_specs=scalar_specs + [matrix_spec] * 4,
        out_specs=[whole(output.shape) for output in outputs],
        out_shape=outputs,
        compiler_params=PARAMS,
        cost_estimate=cost(lines * lines, lines, 8, 8 * 4 * lines * lines),
        name="prepare",
    )(*scalar_arrays, explicit_line, inverse_line, explicit_depth, inverse_depth)

    there = [exchange(first(chunk)) for chunk in range(CHUNKS)]
    back = [exchange(planes([there[chunk]], chunk, [(0, depth)])[0]) for chunk in range(CHUNKS)]
    early, late = [
        [back[chunk][order.index(place)] for chunk, place in blocks] for blocks in arrivals(ranks)
    ]
    return last(late, last_matrices[2:], early_sums(early, last_matrices[:2]))


def oriented(matrix, reflect):
    return jnp.where(reflect == 1, matrix[::-1, ::-1], matrix)


def plain(concentration, species, reaction_rates, levels, sweep_flags,
          explicit_line, inverse_line, explicit_depth, inverse_depth):
    kinetics = (reaction_rates[species[0]], levels[species[0]])
    matmul = functools.partial(jnp.einsum, precision=lax.Precision.HIGHEST)
    line = matmul("ij,jk->ik", inverse_line, explicit_line)
    deep = matmul("ij,jk->ik", inverse_depth, explicit_depth)
    letters = ["ij,jbc->ibc", "ij,ajc->aic", "ij,abj->abi"]

    def sweep(value, step, axis_dim):
        matrix = oriented(deep if axis_dim == 2 else line, sweep_flags[step, axis_dim])
        return matmul(letters[axis_dim], matrix, react(value, kinetics))

    def regroup(value):
        value = lax.all_to_all(value, "row", split_axis=0, concat_axis=1, tiled=True)
        return lax.all_to_all(value, "col", split_axis=0, concat_axis=2, tiled=True)

    def restore(value):
        value = lax.all_to_all(value, "col", split_axis=2, concat_axis=0, tiled=True)
        return lax.all_to_all(value, "row", split_axis=1, concat_axis=0, tiled=True)

    value, home = concentration, True
    for step in range(sweep_flags.shape[0]):
        for axis_dim in [0, 1, 2] if step % 2 == 0 else [2, 1, 0]:
            if home != (axis_dim == 0):
                value = restore(value) if axis_dim == 0 else regroup(value)
                home = axis_dim == 0
            value = sweep(value, step, axis_dim)
    return value if home else restore(value)


def solution(mesh):
    rows, columns = mesh.shape["row"], mesh.shape["col"]
    ranks = rows * columns

    def on_device(*args):
        lines, depth, width = args[0].shape
        fits = (
            args[4].shape[0] == 2
            and ranks & (ranks - 1) == 0
            and ranks >= 2
            and lines % (ranks * CHUNKS * 8) == 0
            and depth % BLOCK == 0
            and width % 128 == 0
            and depth * rows == lines
            and width * columns == args[7].shape[0] == lines
            and 2 * width == lines
        )
        if fits:
            return fast(rows, columns, *args)
        return plain(*args)

    in_specs = (P("groups", "row", "col"), P("groups"), P(), P(), P(), P(), P(), P(), P())
    return jax.shard_map(
        on_device, mesh=mesh, in_specs=in_specs, out_specs=P("groups", "row", "col"), check_vma=False
    )
```

```python
import functools
import jax
import jax.numpy as jnp
from jax import lax
from jax.experimental import pallas as pl
from jax.experimental.pallas import tpu as pltpu
from jax.sharding import PartitionSpec as P

F32 = jnp.float32
BF16 = jnp.bfloat16
CHUNKS = 2
BLOCK = 8
VMEM_LIMIT = 24 * 1024 * 1024
FIRST_LIMIT = 60 * 1024 * 1024
GRAIN = 16
OUT_GRAIN = 4
LATE = 4


def split(value):
    high = value.astype(BF16)
    return high, (value - high.astype(F32)).astype(BF16)


def product(left, right):
    dot = functools.partial(jnp.dot, preferred_element_type=F32)
    return dot(
        jnp.concatenate([left[0], left[1], left[0]], axis=1),
        jnp.concatenate([right[0], right[0], right[1]], axis=0),
    )


def react(value, kinetics):
    rate, level = kinetics
    return value - rate * jnp.tanh(value - level)


def read_kinetics(species_ref, rates_ref, levels_ref):
    index = species_ref[0]
    return rates_ref[index], levels_ref[index]


def relative(index, block, own):
    return ((index // block) ^ own) * block + index % block


def picker(shape, along, source, flag, length):
    wanted = source(lax.broadcasted_iota(jnp.int32, shape, along))
    wanted = jnp.where(flag == 1, length - 1 - wanted, wanted)
    return jnp.where(lax.broadcasted_iota(jnp.int32, shape, 1 - along) == wanted, 1.0, 0.0).astype(BF16)


def combined(inverse, explicit):
    return jnp.dot(inverse, explicit, precision=lax.Precision.HIGHEST, preferred_element_type=F32)


def rearrange(pieces, rows, columns):
    dot = functools.partial(jnp.dot, preferred_element_type=F32)
    return tuple(dot(dot(rows, piece).astype(BF16), columns).astype(BF16) for piece in pieces)


def sending_order(ranks):
    half = ranks // 2
    order = []
    for index in range(half):
        order.append(half + (index ^ (index >> 1) if 2 * index < half else 3 * half // 2 - 1 - index))
        order.append(half - 1 - index)
    return order


def arrivals(ranks):
    order = sending_order(ranks)
    late = order[-1 - LATE : -1]
    early = [(chunk, place) for chunk in range(CHUNKS - 1) for place in order]
    early += [(CHUNKS - 1, place) for place in order if place not in late]
    return early, [(CHUNKS - 1, place) for place in late]


def by_place(refs):
    order = sending_order(len(refs))
    return [refs[order.index(place)] for place in range(len(refs))]


def position():
    return lax.axis_index("row"), lax.axis_index("col")


def first_sweep(chunk, columns, species, rates, levels, flags, explicit, inverse, field, *refs):
    blocks = by_place(refs[:-7])
    held, matrices, done, *small = refs[-7:]
    ranks = len(blocks)
    depth, each, width = blocks[0].shape
    length = field.shape[0]
    row, column = position()
    own = row * columns + column
    targets = [*small, matrices.at[0], matrices.at[1]] + [held.at[cell] for cell in range(depth)]
    sources = [species, rates, levels, flags, inverse, explicit]
    sources += [field.at[:, cell, :] for cell in range(depth)]
    copies = [
        pltpu.make_async_copy(source, target, done.at[index])
        for index, (source, target) in enumerate(zip(sources, targets))
    ]
    for copy in copies:
        copy.start()
    for copy in copies[:-depth]:
        copy.wait()
    species, rates, levels, flags = small
    share = ranks * each
    flag = flags[0, 0]
    matrix = rearrange(
        split(combined(matrices[0], matrices[1])),
        picker((share, length), 0, lambda i: chunk * share + relative(i, each, own), flag, length),
        picker((length, length), 1, lambda i: i, flag, length),
    )
    kinetics = read_kinetics(species, rates, levels)
    for cell in range(0, depth, 2):
        if cell % GRAIN == 0:
            for copy in copies[len(copies) - depth + cell :][:GRAIN]:
                copy.wait()
        value = jnp.concatenate([held[cell], held[cell + 1]], axis=1)
        result = product(matrix, split(react(value, kinetics)))
        for half in range(2):
            piece = result[:, half * width : (half + 1) * width].reshape(ranks, each, width)
            for place in range(ranks):
                blocks[place][cell + half] = piece[place]


def block_sums(blocks, cell, matrix, kinetics):
    value = jnp.concatenate(
        [jnp.concatenate([block[cell + half] for block in blocks], axis=0) for half in range(2)], axis=1
    )
    return product(matrix, split(react(value, kinetics)))


def partial_sums(kinetics, high, low, *refs):
    blocks, out = refs[:-1], refs[-1]
    depth, _, width = out.shape
    for cell in range(0, depth, 2):
        index = pl.program_id(0) * depth + cell
        result = block_sums(blocks, index, (high[...], low[...]), (kinetics[0:1, :], kinetics[1:2, :]))
        out[cell] = result[:, :width]
        out[cell + 1] = result[:, width:]


def last_sweep(kinetics, high, low, *refs):
    blocks, (total, out, held, done) = refs[:-4], refs[-4:]
    depth, _, width = held.shape
    copies = [
        pltpu.make_async_copy(held.at[cell], out.at[:, cell, :], done.at[cell]) for cell in range(depth)
    ]
    for cell in range(0, depth, 2):
        result = block_sums(blocks, cell, (high[...], low[...]), (kinetics[0:1, :], kinetics[1:2, :]))
        held[cell] = result[:, :width] + total[cell]
        held[cell + 1] = result[:, width:] + total[cell + 1]
        if (cell + 2) % OUT_GRAIN == 0:
            for copy in copies[cell + 2 - OUT_GRAIN : cell + 2]:
                copy.start()
    for copy in copies:
        copy.wait()


def prepare(columns, depth, width, each, species, rates, levels, flags, explicit_line, inverse_line,
            explicit_depth, inverse_depth, kinetics, high, low, *last):
    row, column = position()
    rate, level = read_kinetics(species, rates, levels)
    kinetics[0:1, :] = jnp.full((1, kinetics.shape[1]), rate, F32)
    kinetics[1:2, :] = jnp.full((1, kinetics.shape[1]), level, F32)
    line = split(combined(inverse_line[...], explicit_line[...]))
    deep = split(combined(inverse_depth[...], explicit_depth[...]).T)
    shape = line[0].shape
    for place, (pieces, step, axis_dim) in enumerate(
        [(line, 0, 1), (deep, 0, 2), (deep, 1, 2), (line, 1, 1)]
    ):
        own, block = (row, depth) if axis_dim == 1 else (column, width)
        flag = flags[step, axis_dim]
        high[place], low[place] = rearrange(
            pieces,
            *[picker(shape, along, lambda i: relative(i, block, own), flag, shape[0]) for along in range(2)],
        )
    own = row * columns + column
    rows = picker(shape, 0, lambda i: i, flags[1, 0], shape[0])
    for blocks, high, low in zip(arrivals(shape[0] // CHUNKS // each), last[0::2], last[1::2]):

        def source(index):
            cell = index % each
            for number, (chunk, place) in enumerate(blocks):
                start = chunk * (shape[0] // CHUNKS) + (place ^ own) * each
                cell = jnp.where(index // each == number, start + index % each, cell)
            return cell

        selected = (shape[0], len(blocks) * each)
        high[...], low[...] = rearrange(line, rows, picker(selected, 1, source, flags[1, 0], shape[0]))


def plane_sweeps(columns, ranks, kinetics, high, low, *refs):
    refs, field = refs[:-1], refs[-1]
    groups = [by_place(refs[i : i + ranks]) for i in range(0, len(refs), ranks)]
    depths = [group[0].shape[0] for group in groups]
    _, each, width = groups[0][0].shape
    rows = ranks // columns
    depth = high.shape[1] // rows
    splits = next(i for i in range(len(groups)) if sum(depths[:i]) == depth)
    ins, outs = groups[:splits], groups[splits:]
    rate_level = (kinetics[0:1, :], kinetics[1:2, :])
    for place in range(ranks):
        start = place // columns * depth
        lanes = slice(place % columns * width, (place % columns + 1) * width)
        for group in ins:
            for line in range(0, group[place].shape[0], BLOCK):
                field[:, start + line : start + line + BLOCK, lanes] = jnp.swapaxes(
                    group[place][line : line + BLOCK], 0, 1
                )
            start += group[place].shape[0]
    for cell in range(each):
        value = field[cell]
        for place in range(4):
            pieces = split(react(value, rate_level))
            matrix = (high[place], low[place])
            value = product(matrix, pieces) if place in (0, 3) else product(pieces, matrix)
        field[cell] = value
    for place in range(ranks):
        start = place // columns * depth
        lanes = slice(place % columns * width, (place % columns + 1) * width)
        for group in outs:
            for line in range(0, group[place].shape[0], BLOCK):
                group[place][line : line + BLOCK] = jnp.swapaxes(
                    field[:, start + line : start + line + BLOCK, lanes], 0, 1
                )
            start += group[place].shape[0]


PARAMS = pltpu.CompilerParams(vmem_limit_bytes=VMEM_LIMIT)
VMEM = pl.BlockSpec(memory_space=pltpu.VMEM)
HBM = pl.BlockSpec(memory_space=pltpu.HBM)


def scalars(shape):
    return pl.BlockSpec(shape, lambda i: (0,) * len(shape), memory_space=pltpu.SMEM)


def whole(shape):
    return pl.BlockSpec(shape, lambda i: (0,) * len(shape))


def cost(cells, length, sweeps, bytes_accessed):
    return pl.CostEstimate(
        flops=6 * cells * length * sweeps, bytes_accessed=bytes_accessed, transcendentals=cells * sweeps
    )


def fast(rows, columns, concentration, species, reaction_rates, levels, sweep_flags,
         explicit_line, inverse_line, explicit_depth, inverse_depth):
    lines, depth, width = concentration.shape
    ranks = rows * columns
    share = lines // CHUNKS
    each = share // ranks
    size = lines * depth * width
    scalar_arrays = (species, reaction_rates, levels, sweep_flags)
    scalar_specs = [scalars(array.shape) for array in scalar_arrays]
    order = sending_order(ranks)

    def exchange(blocks):
        return [
            lax.ppermute(block, ("row", "col"), [(i, i ^ place) for i in range(ranks)]) if place else block
            for place, block in zip(order, blocks)
        ]

    def block_shapes(count):
        return [jax.ShapeDtypeStruct((count, each, width), F32)] * ranks

    def first(chunk):
        return pl.pallas_call(
            functools.partial(first_sweep, chunk, columns),
            grid=(1,),
            in_specs=[HBM] * 7,
            out_specs=[VMEM] * ranks,
            out_shape=block_shapes(depth),
            scratch_shapes=[
                pltpu.VMEM((depth, lines, width), F32),
                pltpu.VMEM((2, lines, lines), F32),
                pltpu.SemaphoreType.DMA((depth + 2 + len(scalar_arrays),)),
                *[pltpu.SMEM(array.shape, array.dtype) for array in scalar_arrays],
            ],
            compiler_params=pltpu.CompilerParams(vmem_limit_bytes=FIRST_LIMIT),
            cost_estimate=cost(size // CHUNKS, lines, 1, 4 * (size + size // CHUNKS)),
            name=f"first_sweep_{chunk}",
        )(*scalar_arrays, explicit_line, inverse_line, concentration)

    def planes(pieces, chunk, parts):
        outs = pl.pallas_call(
            functools.partial(plane_sweeps, columns, ranks),
            grid=(1,),
            in_specs=[VMEM] * (3 + ranks * len(pieces)),
            out_specs=[VMEM] * (ranks * len(parts)),
            out_shape=[shape for _, count in parts for shape in block_shapes(count)],
            scratch_shapes=[pltpu.VMEM((each, lines, lines), F32)],
            compiler_params=PARAMS,
            cost_estimate=cost(size // CHUNKS, lines, 4, 8 * size // CHUNKS),
            name=f"plane_sweeps_{chunk}",
        )(kinetics, high, low, *[block for blocks in pieces for block in blocks])
        return [outs[i * ranks : (i + 1) * ranks] for i in range(len(parts))]

    def early_sums(blocks, matrix):
        return pl.pallas_call(
            partial_sums,
            grid=(depth // BLOCK,),
            in_specs=[VMEM] * (3 + len(blocks)),
            out_specs=pl.BlockSpec((BLOCK, lines, width), lambda i: (i, 0, 0)),
            out_shape=jax.ShapeDtypeStruct((depth, lines, width), F32),
            compiler_params=PARAMS,
            cost_estimate=cost(size // CHUNKS, lines, 1, 4 * (size + size // CHUNKS)),
            name="partial_sums",
        )(kinetics, *matrix, *blocks)

    def last(blocks, matrix, total):
        return pl.pallas_call(
            last_sweep,
            grid=(1,),
            in_specs=[VMEM] * (4 + len(blocks)),
            out_specs=HBM,
            out_shape=jax.ShapeDtypeStruct((lines, depth, width), F32),
            scratch_shapes=[pltpu.VMEM((depth, lines, width), F32), pltpu.SemaphoreType.DMA((depth,))],
            compiler_params=PARAMS,
            cost_estimate=cost(size // CHUNKS, lines, 1, 4 * (size + size // CHUNKS)),
            name="last_sweep",
        )(kinetics, *matrix, *blocks, total)

    matrix_spec = whole((lines, lines))
    outputs = [
        jax.ShapeDtypeStruct((2, 2 * width), F32),
        *[jax.ShapeDtypeStruct((4, lines, lines), BF16)] * 2,
        *[
            jax.ShapeDtypeStruct((lines, len(blocks) * each), BF16)
            for blocks in arrivals(ranks)
            for _ in range(2)
        ],
    ]
    kinetics, high, low, *last_matrices = pl.pallas_call(
        functools.partial(prepare, columns, depth, width, each),
        grid=(1,),
        in_specs=scalar_specs + [matrix_spec] * 4,
        out_specs=[whole(output.shape) for output in outputs],
        out_shape=outputs,
        compiler_params=PARAMS,
        cost_estimate=cost(lines * lines, lines, 8, 8 * 4 * lines * lines),
        name="prepare",
    )(*scalar_arrays, explicit_line, inverse_line, explicit_depth, inverse_depth)

    there = [exchange(first(chunk)) for chunk in range(CHUNKS)]
    back = [exchange(planes([there[chunk]], chunk, [(0, depth)])[0]) for chunk in range(CHUNKS)]
    early, late = [
        [back[chunk][order.index(place)] for chunk, place in blocks] for blocks in arrivals(ranks)
    ]
    return last(late, last_matrices[2:], early_sums(early, last_matrices[:2]))


def oriented(matrix, reflect):
    return jnp.where(reflect == 1, matrix[::-1, ::-1], matrix)


def plain(concentration, species, reaction_rates, levels, sweep_flags,
          explicit_line, inverse_line, explicit_depth, inverse_depth):
    kinetics = (reaction_rates[species[0]], levels[species[0]])
    matmul = functools.partial(jnp.einsum, precision=lax.Precision.HIGHEST)
    line = matmul("ij,jk->ik", inverse_line, explicit_line)
    deep = matmul("ij,jk->ik", inverse_depth, explicit_depth)
    letters = ["ij,jbc->ibc", "ij,ajc->aic", "ij,abj->abi"]

    def sweep(value, step, axis_dim):
        matrix = oriented(deep if axis_dim == 2 else line, sweep_flags[step, axis_dim])
        return matmul(letters[axis_dim], matrix, react(value, kinetics))

    def regroup(value):
        value = lax.all_to_all(value, "row", split_axis=0, concat_axis=1, tiled=True)
        return lax.all_to_all(value, "col", split_axis=0, concat_axis=2, tiled=True)

    def restore(value):
        value = lax.all_to_all(value, "col", split_axis=2, concat_axis=0, tiled=True)
        return lax.all_to_all(value, "row", split_axis=1, concat_axis=0, tiled=True)

    value, home = concentration, True
    for step in range(sweep_flags.shape[0]):
        for axis_dim in [0, 1, 2] if step % 2 == 0 else [2, 1, 0]:
            if home != (axis_dim == 0):
                value = restore(value) if axis_dim == 0 else regroup(value)
                home = axis_dim == 0
            value = sweep(value, step, axis_dim)
    return value if home else restore(value)


def solution(mesh):
    rows, columns = mesh.shape["row"], mesh.shape["col"]
    ranks = rows * columns

    def on_device(*args):
        lines, depth, width = args[0].shape
        fits = (
            args[4].shape[0] == 2
            and ranks & (ranks - 1) == 0
            and ranks >= 2
            and lines % (ranks * CHUNKS * 8) == 0
            and depth % BLOCK == 0
            and width % 128 == 0
            and depth * rows == lines
            and width * columns == args[7].shape[0] == lines
            and 2 * width == lines
        )
        if fits:
            return fast(rows, columns, *args)
        return plain(*args)

    in_specs = (P("groups", "row", "col"), P("groups"), P(), P(), P(), P(), P(), P(), P())
    return jax.shard_map(
        on_device, mesh=mesh, in_specs=in_specs, out_specs=P("groups", "row", "col"), check_vma=False
    )
```

```python
import functools
import jax
import jax.numpy as jnp
from jax import lax
from jax.experimental import pallas as pl
from jax.experimental.pallas import tpu as pltpu
from jax.sharding import PartitionSpec as P

F32 = jnp.float32
BF16 = jnp.bfloat16
CHUNKS = 2
BLOCK = 8
VMEM_LIMIT = 24 * 1024 * 1024
FIRST_LIMIT = 60 * 1024 * 1024
GRAIN = 16
OUT_GRAIN = 2
LATE = 4


def split(value):
    high = value.astype(BF16)
    return high, (value - high.astype(F32)).astype(BF16)


def product(left, right):
    dot = functools.partial(jnp.dot, preferred_element_type=F32)
    return dot(
        jnp.concatenate([left[0], left[1], left[0]], axis=1),
        jnp.concatenate([right[0], right[0], right[1]], axis=0),
    )


def react(value, kinetics):
    rate, level = kinetics
    return value - rate * jnp.tanh(value - level)


def read_kinetics(species_ref, rates_ref, levels_ref):
    index = species_ref[0]
    return rates_ref[index], levels_ref[index]


def relative(index, block, own):
    return ((index // block) ^ own) * block + index % block


def picker(shape, along, source, flag, length):
    wanted = source(lax.broadcasted_iota(jnp.int32, shape, along))
    wanted = jnp.where(flag == 1, length - 1 - wanted, wanted)
    return jnp.where(lax.broadcasted_iota(jnp.int32, shape, 1 - along) == wanted, 1.0, 0.0).astype(BF16)


def combined(inverse, explicit):
    return jnp.dot(inverse, explicit, precision=lax.Precision.HIGHEST, preferred_element_type=F32)


def rearrange(pieces, rows, columns):
    dot = functools.partial(jnp.dot, preferred_element_type=F32)
    return tuple(dot(dot(rows, piece).astype(BF16), columns).astype(BF16) for piece in pieces)


def sending_order(ranks):
    half = ranks // 2
    order = []
    for index in range(half):
        order.append(half + (index ^ (index >> 1) if 2 * index < half else 3 * half // 2 - 1 - index))
        order.append(half - 1 - index)
    return order


def arrivals(ranks):
    order = sending_order(ranks)
    late = order[-1 - LATE : -1]
    early = [(chunk, place) for chunk in range(CHUNKS - 1) for place in order]
    early += [(CHUNKS - 1, place) for place in order if place not in late]
    return early, [(CHUNKS - 1, place) for place in late]


def by_place(refs):
    order = sending_order(len(refs))
    return [refs[order.index(place)] for place in range(len(refs))]


def position():
    return lax.axis_index("row"), lax.axis_index("col")


def first_sweep(chunk, columns, species, rates, levels, flags, explicit, inverse, field, *refs):
    blocks = by_place(refs[:-7])
    held, matrices, done, *small = refs[-7:]
    ranks = len(blocks)
    depth, each, width = blocks[0].shape
    length = field.shape[0]
    row, column = position()
    own = row * columns + column
    targets = [*small, matrices.at[0], matrices.at[1]] + [held.at[cell] for cell in range(depth)]
    sources = [species, rates, levels, flags, inverse, explicit]
    sources += [field.at[:, cell, :] for cell in range(depth)]
    copies = [
        pltpu.make_async_copy(source, target, done.at[index])
        for index, (source, target) in enumerate(zip(sources, targets))
    ]
    for copy in copies:
        copy.start()
    for copy in copies[:-depth]:
        copy.wait()
    species, rates, levels, flags = small
    share = ranks * each
    flag = flags[0, 0]
    matrix = rearrange(
        split(combined(matrices[0], matrices[1])),
        picker((share, length), 0, lambda i: chunk * share + relative(i, each, own), flag, length),
        picker((length, length), 1, lambda i: i, flag, length),
    )
    kinetics = read_kinetics(species, rates, levels)
    for cell in range(0, depth, 2):
        if cell % GRAIN == 0:
            for copy in copies[len(copies) - depth + cell :][:GRAIN]:
                copy.wait()
        value = jnp.concatenate([held[cell], held[cell + 1]], axis=1)
        result = product(matrix, split(react(value, kinetics)))
        for half in range(2):
            piece = result[:, half * width : (half + 1) * width].reshape(ranks, each, width)
            for place in range(ranks):
                blocks[place][cell + half] = piece[place]


def block_sums(blocks, cell, matrix, kinetics):
    value = jnp.concatenate(
        [jnp.concatenate([block[cell + half] for block in blocks], axis=0) for half in range(2)], axis=1
    )
    return product(matrix, split(react(value, kinetics)))


def partial_sums(kinetics, high, low, *refs):
    blocks, out = refs[:-1], refs[-1]
    depth, _, width = out.shape
    for cell in range(0, depth, 2):
        index = pl.program_id(0) * depth + cell
        result = block_sums(blocks, index, (high[...], low[...]), (kinetics[0:1, :], kinetics[1:2, :]))
        out[cell] = result[:, :width]
        out[cell + 1] = result[:, width:]


def last_sweep(kinetics, high, low, *refs):
    blocks, (total, out, held, done) = refs[:-4], refs[-4:]
    depth, _, width = held.shape
    copies = [
        pltpu.make_async_copy(held.at[cell], out.at[:, cell, :], done.at[cell]) for cell in range(depth)
    ]
    for cell in range(0, depth, 2):
        result = block_sums(blocks, cell, (high[...], low[...]), (kinetics[0:1, :], kinetics[1:2, :]))
        held[cell] = result[:, :width] + total[cell]
        held[cell + 1] = result[:, width:] + total[cell + 1]
        if (cell + 2) % OUT_GRAIN == 0:
            for copy in copies[cell + 2 - OUT_GRAIN : cell + 2]:
                copy.start()
    for copy in copies:
        copy.wait()


def prepare(columns, depth, width, each, species, rates, levels, flags, explicit_line, inverse_line,
            explicit_depth, inverse_depth, kinetics, high, low, *last):
    row, column = position()
    rate, level = read_kinetics(species, rates, levels)
    kinetics[0:1, :] = jnp.full((1, kinetics.shape[1]), rate, F32)
    kinetics[1:2, :] = jnp.full((1, kinetics.shape[1]), level, F32)
    line = split(combined(inverse_line[...], explicit_line[...]))
    deep = split(combined(inverse_depth[...], explicit_depth[...]).T)
    shape = line[0].shape
    for place, (pieces, step, axis_dim) in enumerate(
        [(line, 0, 1), (deep, 0, 2), (deep, 1, 2), (line, 1, 1)]
    ):
        own, block = (row, depth) if axis_dim == 1 else (column, width)
        flag = flags[step, axis_dim]
        high[place], low[place] = rearrange(
            pieces,
            *[picker(shape, along, lambda i: relative(i, block, own), flag, shape[0]) for along in range(2)],
        )
    own = row * columns + column
    rows = picker(shape, 0, lambda i: i, flags[1, 0], shape[0])
    for blocks, high, low in zip(arrivals(shape[0] // CHUNKS // each), last[0::2], last[1::2]):

        def source(index):
            cell = index % each
            for number, (chunk, place) in enumerate(blocks):
                start = chunk * (shape[0] // CHUNKS) + (place ^ own) * each
                cell = jnp.where(index // each == number, start + index % each, cell)
            return cell

        selected = (shape[0], len(blocks) * each)
        high[...], low[...] = rearrange(line, rows, picker(selected, 1, source, flags[1, 0], shape[0]))


def plane_sweeps(columns, ranks, kinetics, high, low, *refs):
    refs, field = refs[:-1], refs[-1]
    groups = [by_place(refs[i : i + ranks]) for i in range(0, len(refs), ranks)]
    depths = [group[0].shape[0] for group in groups]
    _, each, width = groups[0][0].shape
    rows = ranks // columns
    depth = high.shape[1] // rows
    splits = next(i for i in range(len(groups)) if sum(depths[:i]) == depth)
    ins, outs = groups[:splits], groups[splits:]
    rate_level = (kinetics[0:1, :], kinetics[1:2, :])
    for place in range(ranks):
        start = place // columns * depth
        lanes = slice(place % columns * width, (place % columns + 1) * width)
        for group in ins:
            for line in range(0, group[place].shape[0], BLOCK):
                field[:, start + line : start + line + BLOCK, lanes] = jnp.swapaxes(
                    group[place][line : line + BLOCK], 0, 1
                )
            start += group[place].shape[0]
    for cell in range(each):
        value = field[cell]
        for place in range(4):
            pieces = split(react(value, rate_level))
            matrix = (high[place], low[place])
            value = product(matrix, pieces) if place in (0, 3) else product(pieces, matrix)
        field[cell] = value
    for place in range(ranks):
        start = place // columns * depth
        lanes = slice(place % columns * width, (place % columns + 1) * width)
        for group in outs:
            for line in range(0, group[place].shape[0], BLOCK):
                group[place][line : line + BLOCK] = jnp.swapaxes(
                    field[:, start + line : start + line + BLOCK, lanes], 0, 1
                )
            start += group[place].shape[0]


PARAMS = pltpu.CompilerParams(vmem_limit_bytes=VMEM_LIMIT)
VMEM = pl.BlockSpec(memory_space=pltpu.VMEM)
HBM = pl.BlockSpec(memory_space=pltpu.HBM)


def scalars(shape):
    return pl.BlockSpec(shape, lambda i: (0,) * len(shape), memory_space=pltpu.SMEM)


def whole(shape):
    return pl.BlockSpec(shape, lambda i: (0,) * len(shape))


def cost(cells, length, sweeps, bytes_accessed):
    return pl.CostEstimate(
        flops=6 * cells * length * sweeps, bytes_accessed=bytes_accessed, transcendentals=cells * sweeps
    )


def fast(rows, columns, concentration, species, reaction_rates, levels, sweep_flags,
         explicit_line, inverse_line, explicit_depth, inverse_depth):
    lines, depth, width = concentration.shape
    ranks = rows * columns
    share = lines // CHUNKS
    each = share // ranks
    size = lines * depth * width
    scalar_arrays = (species, reaction_rates, levels, sweep_flags)
    scalar_specs = [scalars(array.shape) for array in scalar_arrays]
    order = sending_order(ranks)

    def exchange(blocks):
        return [
            lax.ppermute(block, ("row", "col"), [(i, i ^ place) for i in range(ranks)]) if place else block
            for place, block in zip(order, blocks)
        ]

    def block_shapes(count):
        return [jax.ShapeDtypeStruct((count, each, width), F32)] * ranks

    def first(chunk):
        return pl.pallas_call(
            functools.partial(first_sweep, chunk, columns),
            grid=(1,),
            in_specs=[HBM] * 7,
            out_specs=[VMEM] * ranks,
            out_shape=block_shapes(depth),
            scratch_shapes=[
                pltpu.VMEM((depth, lines, width), F32),
                pltpu.VMEM((2, lines, lines), F32),
                pltpu.SemaphoreType.DMA((depth + 2 + len(scalar_arrays),)),
                *[pltpu.SMEM(array.shape, array.dtype) for array in scalar_arrays],
            ],
            compiler_params=pltpu.CompilerParams(vmem_limit_bytes=FIRST_LIMIT),
            cost_estimate=cost(size // CHUNKS, lines, 1, 4 * (size + size // CHUNKS)),
            name=f"first_sweep_{chunk}",
        )(*scalar_arrays, explicit_line, inverse_line, concentration)

    def planes(pieces, chunk, parts):
        outs = pl.pallas_call(
            functools.partial(plane_sweeps, columns, ranks),
            grid=(1,),
            in_specs=[VMEM] * (3 + ranks * len(pieces)),
            out_specs=[VMEM] * (ranks * len(parts)),
            out_shape=[shape for _, count in parts for shape in block_shapes(count)],
            scratch_shapes=[pltpu.VMEM((each, lines, lines), F32)],
            compiler_params=PARAMS,
            cost_estimate=cost(size // CHUNKS, lines, 4, 8 * size // CHUNKS),
            name=f"plane_sweeps_{chunk}",
        )(kinetics, high, low, *[block for blocks in pieces for block in blocks])
        return [outs[i * ranks : (i + 1) * ranks] for i in range(len(parts))]

    def early_sums(blocks, matrix):
        return pl.pallas_call(
            partial_sums,
            grid=(depth // BLOCK,),
            in_specs=[VMEM] * (3 + len(blocks)),
            out_specs=pl.BlockSpec((BLOCK, lines, width), lambda i: (i, 0, 0)),
            out_shape=jax.ShapeDtypeStruct((depth, lines, width), F32),
            compiler_params=PARAMS,
            cost_estimate=cost(size // CHUNKS, lines, 1, 4 * (size + size // CHUNKS)),
            name="partial_sums",
        )(kinetics, *matrix, *blocks)

    def last(blocks, matrix, total):
        return pl.pallas_call(
            last_sweep,
            grid=(1,),
            in_specs=[VMEM] * (4 + len(blocks)),
            out_specs=HBM,
            out_shape=jax.ShapeDtypeStruct((lines, depth, width), F32),
            scratch_shapes=[pltpu.VMEM((depth, lines, width), F32), pltpu.SemaphoreType.DMA((depth,))],
            compiler_params=PARAMS,
            cost_estimate=cost(size // CHUNKS, lines, 1, 4 * (size + size // CHUNKS)),
            name="last_sweep",
        )(kinetics, *matrix, *blocks, total)

    matrix_spec = whole((lines, lines))
    outputs = [
        jax.ShapeDtypeStruct((2, 2 * width), F32),
        *[jax.ShapeDtypeStruct((4, lines, lines), BF16)] * 2,
        *[
            jax.ShapeDtypeStruct((lines, len(blocks) * each), BF16)
            for blocks in arrivals(ranks)
            for _ in range(2)
        ],
    ]
    kinetics, high, low, *last_matrices = pl.pallas_call(
        functools.partial(prepare, columns, depth, width, each),
        grid=(1,),
        in_specs=scalar_specs + [matrix_spec] * 4,
        out_specs=[whole(output.shape) for output in outputs],
        out_shape=outputs,
        compiler_params=PARAMS,
        cost_estimate=cost(lines * lines, lines, 8, 8 * 4 * lines * lines),
        name="prepare",
    )(*scalar_arrays, explicit_line, inverse_line, explicit_depth, inverse_depth)

    there = [exchange(first(chunk)) for chunk in range(CHUNKS)]
    back = [exchange(planes([there[chunk]], chunk, [(0, depth)])[0]) for chunk in range(CHUNKS)]
    early, late = [
        [back[chunk][order.index(place)] for chunk, place in blocks] for blocks in arrivals(ranks)
    ]
    return last(late, last_matrices[2:], early_sums(early, last_matrices[:2]))


def oriented(matrix, reflect):
    return jnp.where(reflect == 1, matrix[::-1, ::-1], matrix)


def plain(concentration, species, reaction_rates, levels, sweep_flags,
          explicit_line, inverse_line, explicit_depth, inverse_depth):
    kinetics = (reaction_rates[species[0]], levels[species[0]])
    matmul = functools.partial(jnp.einsum, precision=lax.Precision.HIGHEST)
    line = matmul("ij,jk->ik", inverse_line, explicit_line)
    deep = matmul("ij,jk->ik", inverse_depth, explicit_depth)
    letters = ["ij,jbc->ibc", "ij,ajc->aic", "ij,abj->abi"]

    def sweep(value, step, axis_dim):
        matrix = oriented(deep if axis_dim == 2 else line, sweep_flags[step, axis_dim])
        return matmul(letters[axis_dim], matrix, react(value, kinetics))

    def regroup(value):
        value = lax.all_to_all(value, "row", split_axis=0, concat_axis=1, tiled=True)
        return lax.all_to_all(value, "col", split_axis=0, concat_axis=2, tiled=True)

    def restore(value):
        value = lax.all_to_all(value, "col", split_axis=2, concat_axis=0, tiled=True)
        return lax.all_to_all(value, "row", split_axis=1, concat_axis=0, tiled=True)

    value, home = concentration, True
    for step in range(sweep_flags.shape[0]):
        for axis_dim in [0, 1, 2] if step % 2 == 0 else [2, 1, 0]:
            if home != (axis_dim == 0):
                value = restore(value) if axis_dim == 0 else regroup(value)
                home = axis_dim == 0
            value = sweep(value, step, axis_dim)
    return value if home else restore(value)


def solution(mesh):
    rows, columns = mesh.shape["row"], mesh.shape["col"]
    ranks = rows * columns

    def on_device(*args):
        lines, depth, width = args[0].shape
        fits = (
            args[4].shape[0] == 2
            and ranks & (ranks - 1) == 0
            and ranks >= 2
            and lines % (ranks * CHUNKS * 8) == 0
            and depth % BLOCK == 0
            and width % 128 == 0
            and depth * rows == lines
            and width * columns == args[7].shape[0] == lines
            and 2 * width == lines
        )
        if fits:
            return fast(rows, columns, *args)
        return plain(*args)

    in_specs = (P("groups", "row", "col"), P("groups"), P(), P(), P(), P(), P(), P(), P())
    return jax.shard_map(
        on_device, mesh=mesh, in_specs=in_specs, out_specs=P("groups", "row", "col"), check_vma=False
    )
```
